32 devices in a mesh: groups: 2 (over x), zero: 16 (over z, y, core).
Axes of the slice: x: 2, y: 2, z: 4, core: 2. Of those that a mesh axis runs over, the one named last changes fastest.
Arguments:
- features: bfloat16 [8192, 8192], P(('groups', 'zero')), parts along dimension 0, may hold values from -6 to 6
- grad_out: bfloat16 [8192, 1024], P(('groups', 'zero')), parts along dimension 0, may hold values from -6 to 6
- base_weight: bfloat16 [8192, 1024], P('zero'), may hold values from -0.0625 to 0.0625
- factor_a: bfloat16 [16, 8192, 16], P('zero'), may hold values from -0.0625 to 0.0625
- factor_b: bfloat16 [16, 16, 1024], P('zero'), may hold values from -0.1875 to 0.1875
- tenant_ids: int32 [8192], P(('groups', 'zero')), parts along dimension 0, may hold values from 0 to 15, as said below
- owner_of: int32 [16], replicated, may hold values from 0 to 15, as said below
Outputs:
- grad_in: bfloat16 [8192, 8192], P(('groups', 'zero')), parts along dimension 0
- grad_a: float32 [32, 8192, 16], P(('groups', 'zero')), parts along dimension 0
- grad_b: float32 [32, 16, 1024], P(('groups', 'zero')), parts along dimension 0
The draws below stay inside these ranges and needn't reach their ends.
There are 2 independent parts, one for each index of `groups`. The reference program is written for one: setup_inputs(seed, part) draws one part's arguments, and reference() takes and returns one part's arrays. A program takes and returns all parts, laid end to end along the dimension named above; an argument that names none is the same for every part. Nothing has to cross between parts.
Inputs may be any that keep to these rules, and one draw needn't show every extreme that they name: `tenant_ids`: ids are constant on aligned blocks of 128 rows, never fall along the rows of a group, and every tenant has at least one block. `owner_of`: every device index owns the same number of tenants, 1.
All inputs are finite; a program needn't handle non-finite values.
Results may differ from the reference program's by a relative error of at most 0.0034.
Values may be sent and summed in bfloat16 or wider, within the bound.
A program may use at most 128 MiB of HBM per device.

```python
import jax
import jax.numpy as jnp
from jax import lax

D = 8192
DKV = 1024
R = 16
BLK = 128
TEN_DEV = 1
TENANTS = 16
TOKENS = 4096


def draw_tenant_ids(key, part):
    key = jax.random.fold_in(key, 11)
    first_key, second_key = jax.random.split(key)
    block_total = TOKENS // BLK
    extra = block_total - TENANTS
    left = jax.random.randint(first_key, (extra,), 0, TENANTS)
    right = jax.random.randint(second_key, (extra,), 0, TENANTS)
    popular = (left * right // TENANTS).astype(jnp.int32)
    every = jnp.concatenate([jnp.arange(TENANTS, dtype=jnp.int32), popular])
    return jnp.repeat(jnp.sort(every), BLK).astype(jnp.int32)


def draw_owner_of(key, part):
    key = jax.random.fold_in(key, 23)
    return (jax.random.permutation(key, TENANTS) // TEN_DEV).astype(jnp.int32)


def level_of(own_key, shape, shards, smallest, largest):
    factor_of, own = 1.0, jax.random.fold_in(own_key, 6)
    for axis_at, blocks in shards:
        draws = jnp.exp(jax.random.uniform(jax.random.fold_in(own, axis_at), (blocks,), jnp.float32, smallest / len(shards), largest / len(shards)))
        factor_of = factor_of * jnp.repeat(draws, shape[axis_at] // blocks).reshape([-1 if axis == axis_at else 1 for axis in range(len(shape))])
    return factor_of


def noise(own_key, extent, width, most, cuts=(), held_as=jnp.bfloat16):
    factor_of = level_of(own_key, extent, cuts, -0.22, 0.18) if cuts else 1.0
    result = jax.random.normal(own_key, extent, jnp.float32) * width * factor_of
    return jnp.minimum(jnp.maximum(result, -most), most).astype(held_as)


def setup_inputs(seed: int = 0, part: int = 0) -> dict:
    arg_keys = jax.random.split(jax.random.key(seed), 8)
    part_keys = jax.random.split(jax.random.fold_in(arg_keys[7], part), 8)
    features = noise(part_keys[0], (TOKENS, D), 1.0, 6.0, ((0, 16),))
    grad_out = noise(part_keys[1], (TOKENS, DKV), 1.0, 6.0, ((0, 16),))
    base_weight = noise(arg_keys[2], (D, DKV), D ** -0.5, 0.0625, ((0, 16),))
    factor_a = noise(arg_keys[3], (TENANTS, D, R), D ** -0.5, 0.0625, ((0, 16),))
    factor_b = noise(arg_keys[4], (TENANTS, R, DKV), DKV ** -0.5, 0.1875, ((0, 16),))
    tenant_ids = draw_tenant_ids(jax.random.fold_in(jax.random.fold_in(arg_keys[7], part), 71), part)
    owner_of = draw_owner_of(jax.random.fold_in(arg_keys[7], 71), part)
    return {"features": features, "grad_out": grad_out, "base_weight": base_weight, "factor_a": factor_a, "factor_b": factor_b, "tenant_ids": tenant_ids, "owner_of": owner_of}


low_rank_scale = 2.0


def slot_table(owner_of):
    tenant_count = owner_of.shape[0]
    positions = jnp.arange(tenant_count, dtype=jnp.int32)
    before = (owner_of[None, :] == owner_of[:, None]) & (positions[None, :] < positions[:, None])
    return (owner_of * TEN_DEV + jnp.sum(before.astype(jnp.int32), axis=1)).astype(jnp.int32)


def reference(features, grad_out, base_weight, factor_a, factor_b, tenant_ids, owner_of):
    block_count = TOKENS // BLK
    block_ids = tenant_ids.reshape(block_count, BLK)[:, 0]
    slots = slot_table(owner_of)
    block_slot = slots[block_ids]
    a_blocks = factor_a[block_slot].astype(jnp.float32)
    b_blocks = factor_b[block_slot].astype(jnp.float32)
    blocked_in = features.reshape(block_count, BLK, D).astype(jnp.float32)
    blocked_out = grad_out.reshape(block_count, BLK, DKV).astype(jnp.float32)
    low_proj = (low_rank_scale * jnp.einsum("nrk,njk->nrj", blocked_out, b_blocks)).astype(jnp.bfloat16)
    low_wide = low_proj.astype(jnp.float32)
    correction = jnp.einsum("nrj,ndj->nrd", low_wide, a_blocks).reshape(TOKENS, D)
    base = jnp.dot(grad_out, base_weight.T, preferred_element_type=jnp.float32)
    grad_in = (base + correction).astype(jnp.bfloat16)
    inner = jnp.einsum("nrd,ndj->nrj", blocked_in, a_blocks).astype(jnp.bfloat16).astype(jnp.float32)
    part_a = jnp.einsum("nrd,nrj->ndj", blocked_in, low_wide)
    part_b = low_rank_scale * jnp.einsum("nrj,nrk->njk", inner, blocked_out)
    targets = jnp.arange(TENANTS, dtype=jnp.int32)
    member = (block_slot[None, :] == targets[:, None]).astype(jnp.float32)
    counts = BLK * jnp.sum(member, axis=1)
    shares = member / counts[:, None]
    grad_a = jnp.dot(shares, part_a.reshape(block_count, D * R), precision=lax.Precision.HIGHEST).reshape(TENANTS, D, R)
    grad_b = jnp.dot(shares, part_b.reshape(block_count, R * DKV), precision=lax.Precision.HIGHEST).reshape(TENANTS, R, DKV)
    return grad_in, grad_a, grad_b
```

```python
import functools

import jax
import jax.numpy as jnp
from jax import lax
from jax.experimental import pallas as pl
from jax.experimental.pallas import tpu as pltpu
from jax.sharding import PartitionSpec as P

BLK = 128
LANES = 128
low_rank_scale = 2.0
MESH = pl.DeviceIdType.MESH
NT = (((1,), (1,)), ((), ()))
TN = (((0,), (0,)), ((), ()))
CW, CCW, ACROSS, SIB_CW, SIB_CCW, SIB_ACROSS, SIB_OWN = range(7)


def slot_table(owner_of):
    tenant_count = owner_of.shape[0]
    positions = jnp.arange(tenant_count, dtype=jnp.int32)
    before = (owner_of[None, :] == owner_of[:, None]) & (positions[None, :] < positions[:, None])
    return owner_of + jnp.sum(before.astype(jnp.int32), axis=1)


def chip_at(pos, chips):
    if chips == 8:
        return 2 * pos + (pos // 4) * (15 - 4 * pos)
    return pos


def pos_of(chip, chips):
    if chips == 8:
        z, y = chip // 2, chip % 2
        return z + y * (7 - 2 * z)
    return chip


class Gather:
    def __init__(self, where, region, send, recv):
        self.where, self.region, self.send, self.recv = where, region, send, recv
        self.started, self.received = [], set()

    def copy(self, kind, s):
        g, across, r, core, me, sib, n = self.where
        if kind == SIB_OWN:
            pos, part = r, None
        elif kind == CW:
            pos, part = r - s + n, 0
        elif kind == CCW:
            pos, part = r + s, 1
        elif kind in (ACROSS, SIB_CW):
            pos, part = r - 1 - s + n, 0
        elif kind == SIB_CCW:
            pos, part = r + 1 + s, 1
        else:
            pos, part = r - 1 - s + n, 2
        if kind == CW:
            to = (g, chip_at((r + 1) % n, n) * 2 + core)
        elif kind == CCW:
            to = (g, chip_at((r + n - 1) % n, n) * 2 + core)
        elif kind == ACROSS:
            to = (across, me)
        else:
            to = (g, sib)
        ref = self.region(chip_at(pos % n, n) * 2 + core, part)
        return pltpu.make_async_remote_copy(
            src_ref=ref,
            dst_ref=ref,
            send_sem=self.send.at[kind, s],
            recv_sem=self.recv.at[kind, s],
            device_id=to,
            device_id_type=MESH,
        )

    def start(self, kind, s):
        self.copy(kind, s).start()
        self.started.append((kind, s))

    def need(self, kind, s):
        if (kind, s) not in self.received:
            self.received.add((kind, s))
            self.copy(kind, s).wait_recv()

    def begin(self):
        self.start(CW, 0)
        self.start(CCW, 0)
        self.start(SIB_OWN, 0)

    def step(self, s):
        n = self.where[-1]
        self.need(CW, s)
        if s < n - 2:
            self.start(CW, s + 1)
        self.start(ACROSS, s)
        self.start(SIB_CW, s)
        self.need(CCW, s)
        if s < n - 2:
            self.start(CCW, s + 1)
        self.start(SIB_CCW, s)
        if s >= 1:
            self.need(ACROSS, s - 1)
            self.start(SIB_ACROSS, s - 1)
        if s == n - 2:
            self.need(ACROSS, s)
            self.start(SIB_ACROSS, s)

    def whole(self, d):
        n = self.where[-1]
        if d == 0:
            self.need(SIB_OWN, 0)
        else:
            for own, other, s in (
                (CW, SIB_CW, d - 1),
                (CCW, SIB_CCW, n - 1 - d),
                (ACROSS, SIB_ACROSS, d - 1),
            ):
                self.need(own, s)
                self.need(other, s)

    def end(self):
        for kind, s in self.started:
            self.copy(kind, s).wait_send()


def kernel(
    zero, slots, feat_in, go, w_in, at_in, b_in, gi, ga, gb,
    feat, out, wg, abg, a_sel, low, sent, got, summed, final,
    load, stored, w_send, w_recv, ab_send, ab_recv, p_send, p_recv, f_send, f_recv,
):
    g, me = lax.axis_index("groups"), lax.axis_index("zero")
    n = zero // 2
    core = me % 2
    sib = me + 1 - 2 * core
    parity = g % 2
    across = g + 1 - 2 * parity
    r = pos_of(me // 2, n)
    rows, width = feat.shape
    blocks = rows // BLK
    rank = at_in.shape[0]
    kv = b_in.shape[1]
    held = w_in.shape[0]
    picked = blocks * rank
    piece = width // zero
    tenants = zero

    loads = [
        pltpu.make_async_copy(at_in, abg.at[me, :, pl.ds(0, width)], load.at[0]),
        pltpu.make_async_copy(b_in, abg.at[me, :, pl.ds(width, kv)], load.at[1]),
        pltpu.make_async_copy(w_in, wg.at[me], load.at[2]),
        pltpu.make_async_copy(feat_in, feat, load.at[3]),
    ]
    for copy in loads:
        copy.start()

    barrier = pltpu.get_barrier_semaphore()
    pl.semaphore_signal(barrier, inc=1, device_id=(across, me), device_id_type=MESH)

    def greet(i, c):
        pl.semaphore_signal(
            barrier, inc=1, device_id=(g, (me + i) % zero), device_id_type=MESH
        )
        return c

    lax.fori_loop(1, zero, greet, 0)
    pl.semaphore_wait(barrier, zero)

    w_third = -(-held // 48) * 16
    ab_third = -(-(width + kv) // (3 * LANES)) * LANES

    def cut(total, third, part, unit):
        if part == 1:
            return pl.ds(third, total - 2 * third)
        at = (parity if part == 0 else 1 - parity) * (total - third)
        return pl.ds(pl.multiple_of(at, unit), third)

    def w_region(i, part):
        return wg.at[i] if part is None else wg.at[i, cut(held, w_third, part, 16), :]

    def ab_region(i, part):
        if part is None:
            return abg.at[i]
        return abg.at[i, :, cut(width + kv, ab_third, part, LANES)]

    where = (g, across, r, core, me, sib, n)
    ab = Gather(where, ab_region, ab_send, ab_recv)
    w = Gather(where, w_region, w_send, w_recv)

    loads[0].wait()
    loads[1].wait()
    ab.begin()
    loads[2].wait()
    w.begin()
    for s in range(n - 1):
        ab.step(s)
        if s == n // 2:
            w.step(0)
    for d in range(n):
        ab.whole(d)

    row = lax.broadcasted_iota(jnp.int32, (rows, picked), 0) // BLK
    col = lax.broadcasted_iota(jnp.int32, (rows, picked), 1) // rank
    mine = row == col
    tag = jnp.zeros((picked, LANES), jnp.float32)
    at = lax.broadcasted_iota(jnp.int32, (picked, LANES), 0) // rank
    b_parts = []
    for k in range(blocks):
        slot = slots[k]
        a_sel[k * rank : (k + 1) * rank, :] = abg[slot, :, 0:width]
        b_parts.append(abg[slot, :, width : width + kv])
        tag = jnp.where(at == k, slot.astype(jnp.float32), tag)
    tag = tag.astype(jnp.bfloat16)
    b_sel = jnp.concatenate(b_parts, axis=0)
    wide = low_rank_scale * lax.dot_general(go[...], b_sel, NT, preferred_element_type=jnp.float32)
    low[...] = jnp.where(mine, wide, 0.0).astype(jnp.bfloat16)
    loads[3].wait()

    def parts(p, inner):
        cols = pl.ds(pl.multiple_of(p * piece, piece), piece)
        x = feat[:, cols]
        part = lax.dot_general(low[...], x, TN, preferred_element_type=jnp.float32)
        sent[p, :, 0:piece] = part.astype(jnp.bfloat16)
        sent[p, :, piece + LANES : piece + 2 * LANES] = tag
        return inner + lax.dot_general(x, a_sel[:, cols], NT, preferred_element_type=jnp.float32)

    inner = lax.fori_loop(0, zero, parts, jnp.zeros((rows, picked), jnp.float32))
    w.step(1)
    inner = jnp.where(mine, inner, 0.0).astype(jnp.bfloat16)
    part_b = low_rank_scale * lax.dot_general(
        inner, go[...], TN, preferred_element_type=jnp.float32
    )
    part_b = part_b.astype(jnp.bfloat16)
    again = zero // (kv // LANES)
    for p in range(zero):
        c = p // again
        sent[p, :, piece : piece + LANES] = part_b[:, c * LANES : (c + 1) * LANES]

    def part_copy(i):
        to = (me + i) % zero
        return pltpu.make_async_remote_copy(
            src_ref=sent.at[to], dst_ref=got.at[me], send_sem=p_send.at[i],
            recv_sem=p_recv.at[i], device_id=(g, to), device_id_type=MESH,
        )

    def final_copy(i):
        to = (me + i) % zero
        return pltpu.make_async_remote_copy(
            src_ref=summed.at[to], dst_ref=final.at[me], send_sem=f_send.at[i],
            recv_sem=f_recv.at[i], device_id=(g, to), device_id_type=MESH,
        )

    def each(act):
        def go_on(i, c):
            act(i)
            return c

        lax.fori_loop(1, zero, go_on, 0)

    each(lambda i: part_copy(i).start())
    got[me] = sent[me]

    def base(d, order):
        def one(k, c):
            z = chip_at((r - d + n) % n, n) * 2 + k
            cols = pl.ds(pl.multiple_of(z * held, held), held)
            total = lax.dot_general(go[...], wg[z], NT, preferred_element_type=jnp.float32)
            total += jnp.dot(low[...], a_sel[:, cols], preferred_element_type=jnp.float32)
            out[:, cols] = total.astype(jnp.bfloat16)
            pltpu.make_async_copy(out.at[:, cols], gi.at[:, cols], stored.at[2 * order + k]).start()
            return c

        w.whole(d)
        lax.fori_loop(0, 2, one, 0)

    def add_up():
        each(lambda i: part_copy(i).wait_recv())
        total = zero * picked
        sources = got[...].reshape(total, piece + 2 * LANES)
        tags = sources[:, piece + LANES :].astype(jnp.float32)
        values = sources[:, : piece + LANES]
        r_at = lax.broadcasted_iota(jnp.int32, (total, LANES), 0) % rank
        l_at = lax.broadcasted_iota(jnp.int32, (total, LANES), 1)
        same = r_at == l_at % rank
        per = LANES // rank
        for e in range(tenants // per):
            targets = (l_at // rank + e * per).astype(jnp.float32)
            member = jnp.where(same & (tags == targets), 1.0, 0.0).astype(jnp.bfloat16)
            sums = lax.dot_general(member, values, TN, preferred_element_type=jnp.float32)
            count = lax.dot_general(
                member, jnp.ones((total, LANES), jnp.bfloat16), TN,
                preferred_element_type=jnp.float32,
            )
            sums = sums / (BLK * count[:, 0:1])
            summed[e * per : (e + 1) * per] = sums.reshape(per, rank, piece + LANES)
        each(lambda i: final_copy(i).start())
        final[me] = summed[me]

    base(0, 0)
    order, ready = 1, []
    for s in range(2, n - 1):
        w.step(s)
        if s == 3:
            add_up()
        for d in ready:
            base(d, order)
            order += 1
        ready = sorted({d for d in (s + 1, n - 1 - s) if 2 * s + 2 >= n})
    for d in ready:
        base(d, order)
        order += 1

    each(lambda i: final_copy(i).wait_recv())
    for p in range(zero):
        ga[:, p * piece : (p + 1) * piece] = final[p, :, 0:piece]
    for c in range(kv // LANES):
        gb[:, c * LANES : (c + 1) * LANES] = final[c * again, :, piece : piece + LANES]
    ab.end()
    w.end()
    each(lambda i: part_copy(i).wait_send())
    each(lambda i: final_copy(i).wait_send())

    def written(i, c):
        cols = pl.ds(pl.multiple_of(i * held, held), held)
        pltpu.make_async_copy(out.at[:, cols], gi.at[:, cols], stored.at[i]).wait()
        return c

    lax.fori_loop(0, zero, written, 0)


def body(features, grad_out, base_weight, factor_a, factor_b, tenant_ids, owner_of):
    zero = lax.axis_size("zero")
    rows, width = features.shape
    kv = grad_out.shape[1]
    rank = factor_a.shape[2]
    held = base_weight.shape[0]
    blocks = rows // BLK
    piece = width // zero
    picked = blocks * rank
    n = zero // 2
    slots = jnp.take(slot_table(owner_of), tenant_ids.reshape(blocks, BLK)[:, 0])
    bf16, f32 = jnp.bfloat16, jnp.float32
    vmem = pl.BlockSpec(memory_space=pltpu.VMEM)
    anywhere = pl.BlockSpec(memory_space=pl.ANY)
    dma = pltpu.SemaphoreType.DMA
    grad_in, grad_at, grad_b = pl.pallas_call(
        functools.partial(kernel, zero),
        out_shape=(
            jax.ShapeDtypeStruct((rows, width), bf16),
            jax.ShapeDtypeStruct((rank, width), f32),
            jax.ShapeDtypeStruct((rank, kv), f32),
        ),
        in_specs=[
            pl.BlockSpec(memory_space=pltpu.SMEM), anywhere, vmem, anywhere, anywhere, anywhere,
        ],
        out_specs=(anywhere, vmem, vmem),
        scratch_shapes=[
            pltpu.VMEM((rows, width), bf16),
            pltpu.VMEM((rows, width), bf16),
            pltpu.VMEM((zero, held, kv), bf16),
            pltpu.VMEM((zero, rank, width + kv), bf16),
            pltpu.VMEM((picked, width), bf16),
            pltpu.VMEM((rows, picked), bf16),
            pltpu.VMEM((zero, picked, piece + 2 * LANES), bf16),
            pltpu.VMEM((zero, picked, piece + 2 * LANES), bf16),
            pltpu.VMEM((zero, rank, piece + LANES), f32),
            pltpu.VMEM((zero, rank, piece + LANES), f32),
            dma((4,)),
            dma((zero,)),
            dma((7, n - 1)),
            dma((7, n - 1)),
            dma((7, n - 1)),
            dma((7, n - 1)),
            dma((zero,)),
            dma((zero,)),
            dma((zero,)),
            dma((zero,)),
        ],
        compiler_params=pltpu.CompilerParams(
            collective_id=0, has_side_effects=True, vmem_limit_bytes=58 * 2**20
        ),
        cost_estimate=pl.CostEstimate(
            flops=2 * rows * width * (kv + 3 * picked),
            bytes_accessed=2 * (2 * rows * width + width * kv),
            transcendentals=0,
        ),
    )(
        slots,
        features,
        grad_out,
        base_weight,
        jnp.swapaxes(factor_a[0], 0, 1),
        factor_b[0],
    )
    return grad_in, jnp.swapaxes(grad_at, 0, 1)[None], grad_b[None]


def solution(mesh):
    placed = (
        P(("groups", "zero"), None),
        P(("groups", "zero"), None),
        P("zero", None),
        P("zero", None, None),
        P("zero", None, None),
        P(("groups", "zero")),
        P(),
    )
    return jax.shard_map(
        body,
        mesh=mesh,
        in_specs=placed,
        out_specs=(
            P(("groups", "zero"), None),
            P(("groups", "zero"), None, None),
            P(("groups", "zero"), None, None),
        ),
        check_vma=False,
    )
```

```python
import functools

import jax
import jax.numpy as jnp
from jax import lax
from jax.experimental import pallas as pl
from jax.experimental.pallas import tpu as pltpu
from jax.sharding import PartitionSpec as P

BLK = 128
LANES = 128
low_rank_scale = 2.0
MESH = pl.DeviceIdType.MESH
NT = (((1,), (1,)), ((), ()))
TN = (((0,), (0,)), ((), ()))
PLAN = {"cuts": 4, "after": (2, 2, 2, 2), "add": 4}
CW, CCW, ACROSS_CW, ACROSS_CCW, SIB_CW, SIB_CCW, SIB_ACROSS_CW, SIB_ACROSS_CCW, OWN = range(9)


def slot_of(tenant, owner_of):
    owner = owner_of[tenant]

    def count(u, slot):
        return slot + jnp.where((owner_of[u] == owner) & (u < tenant), 1, 0)

    return lax.fori_loop(0, owner_of.shape[0], count, owner)


def chip_at(pos, chips):
    if chips == 8:
        return 2 * pos + (pos // 4) * (15 - 4 * pos)
    return pos


def pos_of(chip, chips):
    if chips == 8:
        z, y = chip // 2, chip % 2
        return z + y * (7 - 2 * z)
    return chip


class Gather:
    def __init__(self, where, region, send, recv):
        self.where, self.region, self.send, self.recv = where, region, send, recv
        self.half = where[-1] // 2
        self.started, self.received = [], set()

    def copy(self, kind, s):
        g, across, r, core, me, sib, n = self.where
        ahead = 1 - 2 * core
        way = -ahead if kind in (CW, ACROSS_CW, SIB_CW, SIB_ACROSS_CW) else ahead
        back = kind in (CCW, SIB_CCW)
        if kind == OWN:
            pos, part, to = r, None, (g, sib)
        elif kind in (CW, CCW):
            pos = r + s * way
            to = (g, chip_at((r - way + n) % n, n) * 2 + core)
        else:
            pos = r + (1 + s) * way
            to = (across, me) if kind in (ACROSS_CW, ACROSS_CCW) else (g, sib)
        if kind in (CW, CCW, SIB_CW, SIB_CCW):
            part = (1 if back else 0) if s == self.half - 1 else 3
        elif kind in (ACROSS_CW, ACROSS_CCW):
            part = 0
        elif kind != OWN:
            part = 2
        ref = self.region(chip_at((pos + n) % n, n) * 2 + core, part)
        return pltpu.make_async_remote_copy(
            src_ref=ref,
            dst_ref=ref,
            send_sem=self.send.at[kind, s],
            recv_sem=self.recv.at[kind, s],
            device_id=to,
            device_id_type=MESH,
        )

    def start(self, kind, s):
        self.copy(kind, s).start()
        self.started.append((kind, s))

    def need(self, kind, s):
        if (kind, s) not in self.received:
            self.received.add((kind, s))
            self.copy(kind, s).wait_recv()

    def begin(self):
        self.start(CW, 0)
        self.start(CCW, 0)
        self.start(OWN, 0)

    def step(self, s):
        last = s == self.half - 1
        for kind in (CW, CCW):
            self.need(kind, s)
            if not last:
                self.start(kind, s + 1)
            if kind == CW or not last:
                self.start(ACROSS_CW + kind, s)
            self.start(SIB_CW + kind, s)
        if s >= 1:
            self.pass_on(s - 1, (CW, CCW))
        if last:
            self.pass_on(s, (CW,))

    def pass_on(self, s, kinds):
        for kind in kinds:
            self.need(ACROSS_CW + kind, s)
            self.start(SIB_ACROSS_CW + kind, s)

    def whole(self, d):
        half, n = self.half, self.where[-1]
        if d == 0:
            needs = [(OWN, 0)]
        elif d == half:
            needs = [(k, half - 1) for k in (CW, CCW, ACROSS_CW, SIB_CW, SIB_CCW, SIB_ACROSS_CW)]
        elif d < half:
            needs = [(k, d - 1) for k in (CW, ACROSS_CW, SIB_CCW, SIB_ACROSS_CCW)]
        else:
            needs = [(k, n - d - 1) for k in (CCW, ACROSS_CCW, SIB_CW, SIB_ACROSS_CW)]
        for need in needs:
            self.need(*need)

    def end(self):
        for kind, s in self.started:
            self.copy(kind, s).wait_send()


def kernel(
    zero, plan, tenant_ids, owner_of, feat_in, go, w_in, at_in, b_in, gi, ga, gb,
    feat, out, wg, abg, a_sel, low, sent, got, summed, final,
    load, stored, w_send, w_recv, ab_send, ab_recv, p_send, p_recv, f_send, f_recv,
):
    g, me = lax.axis_index("groups"), lax.axis_index("zero")
    n = zero // 2
    core = me % 2
    sib = me + 1 - 2 * core
    parity = g % 2
    across = g + 1 - 2 * parity
    r = pos_of(me // 2, n)
    rows, width = feat.shape
    blocks = rows // BLK
    rank = at_in.shape[0]
    kv = b_in.shape[1]
    held = w_in.shape[0]
    picked = blocks * rank
    piece = width // zero
    tenants = zero

    loads = [
        pltpu.make_async_copy(at_in, abg.at[me, :, pl.ds(0, width)], load.at[0]),
        pltpu.make_async_copy(b_in, abg.at[me, :, pl.ds(width, kv)], load.at[1]),
        pltpu.make_async_copy(w_in, wg.at[me], load.at[2]),
        pltpu.make_async_copy(feat_in, feat, load.at[3]),
    ]
    for copy in loads:
        copy.start()

    barrier = pltpu.get_barrier_semaphore()
    pl.semaphore_signal(barrier, inc=1, device_id=(across, me), device_id_type=MESH)

    def greet(i, c):
        pl.semaphore_signal(
            barrier, inc=1, device_id=(g, (me + i) % zero), device_id_type=MESH
        )
        return c

    lax.fori_loop(1, zero, greet, 0)
    pl.semaphore_wait(barrier, zero)

    cuts = plan["cuts"]
    sub = held // cuts
    w_third = -(-sub * 3 // 128) * 16
    ab_third = (width + kv) * 3 // (8 * LANES) * LANES

    def cut(total, third, part, unit):
        if part == 1:
            return pl.ds(third, total - 2 * third)
        if part == 3:
            return pl.ds(pl.multiple_of(parity * third, unit), total - third)
        at = (parity if part == 0 else 1 - parity) * (total - third)
        return pl.ds(pl.multiple_of(at, unit), third)

    def w_region(e, i, part):
        if part is None:
            return wg.at[i, pl.ds(e * sub, sub), :]
        rows_of = cut(sub, w_third, part, 16)
        return wg.at[i, pl.ds(pl.multiple_of(e * sub + rows_of.start, 16), rows_of.size), :]

    def ab_region(i, part):
        if part is None:
            return abg.at[i]
        return abg.at[i, :, cut(width + kv, ab_third, part, LANES)]

    where = (g, across, r, core, me, sib, n)
    ab = Gather(where, ab_region, ab_send, ab_recv)
    ws = [
        Gather(where, functools.partial(w_region, e), w_send.at[e], w_recv.at[e])
        for e in range(cuts)
    ]

    loads[0].wait()
    loads[1].wait()
    ab.begin()
    loads[2].wait()
    for w in ws:
        w.begin()
    turns = [(s, e) for s in range(n // 2) for e in range(cuts)]
    after = plan["after"]
    for s in range(n // 2):
        ab.step(s)
        for _ in range(after[s] if s < len(after) else 0):
            t, e = turns.pop(0)
            ws[e].step(t)
    for d in range(n):
        ab.whole(d)

    def advance():
        s, e = turns.pop(0)
        ws[e].step(s)

    row = lax.broadcasted_iota(jnp.int32, (rows, picked), 0) // BLK
    col = lax.broadcasted_iota(jnp.int32, (rows, picked), 1) // rank
    mine = row == col
    tag = jnp.zeros((picked, LANES), jnp.float32)
    at = lax.broadcasted_iota(jnp.int32, (picked, LANES), 0) // rank
    b_parts = []
    for k in range(blocks):
        slot = slot_of(tenant_ids[k * BLK], owner_of)
        a_sel[k * rank : (k + 1) * rank, :] = abg[slot, :, 0:width]
        b_parts.append(abg[slot, :, width : width + kv])
        tag = jnp.where(at == k, slot.astype(jnp.float32), tag)
    b_sel = jnp.concatenate(b_parts, axis=0)
    wide = low_rank_scale * lax.dot_general(go[...], b_sel, NT, preferred_element_type=jnp.float32)
    low[...] = jnp.where(mine, wide, 0.0).astype(jnp.bfloat16)
    loads[3].wait()

    def parts(p, inner):
        cols = pl.ds(pl.multiple_of(p * piece, piece), piece)
        x = feat[:, cols]
        part = lax.dot_general(low[...], x, TN, preferred_element_type=jnp.float32)
        sent[p, :, 0:piece] = part.astype(jnp.bfloat16)
        return inner + lax.dot_general(x, a_sel[:, cols], NT, preferred_element_type=jnp.float32)

    inner = lax.fori_loop(0, zero, parts, jnp.zeros((rows, picked), jnp.float32))
    advance()
    inner = jnp.where(mine, inner, 0.0).astype(jnp.bfloat16)
    part_b = low_rank_scale * lax.dot_general(
        inner, go[...], TN, preferred_element_type=jnp.float32
    )
    again = zero // (kv // LANES)
    lane = lax.broadcasted_iota(jnp.int32, (picked, LANES), 1) * again // LANES
    for p in range(zero):
        c = p // again
        chunk = jnp.where(lane == p % again, part_b[:, c * LANES : (c + 1) * LANES], tag)
        sent[p, :, piece : piece + LANES] = chunk.astype(jnp.bfloat16)

    def part_copy(i):
        to = (me + i) % zero
        return pltpu.make_async_remote_copy(
            src_ref=sent.at[to], dst_ref=got.at[me], send_sem=p_send.at[i],
            recv_sem=p_recv.at[i], device_id=(g, to), device_id_type=MESH,
        )

    def final_copy(i):
        to = (me + i) % zero
        return pltpu.make_async_remote_copy(
            src_ref=summed.at[to], dst_ref=final.at[me], send_sem=f_send.at[i],
            recv_sem=f_recv.at[i], device_id=(g, to), device_id_type=MESH,
        )

    def each(act):
        def go_on(i, c):
            act(i)
            return c

        lax.fori_loop(1, zero, go_on, 0)

    each(lambda i: part_copy(i).start())
    got[me] = sent[me]

    made = []

    def base(d, order):
        def one(k, c):
            z = chip_at((r - d * (1 - 2 * core) + n) % n, n) * 2 + k
            cols = pl.ds(pl.multiple_of(z * held, held), held)
            total = lax.dot_general(go[...], wg[z], NT, preferred_element_type=jnp.float32)
            total += jnp.dot(low[...], a_sel[:, cols], preferred_element_type=jnp.float32)
            out[:, cols] = total.astype(jnp.bfloat16)
            pltpu.make_async_copy(out.at[:, cols], gi.at[:, cols], stored.at[2 * order + k]).start()
            return c

        made.append(d)
        for w in ws:
            w.whole(d)
        lax.fori_loop(0, 2, one, 0)

    def add_up():
        each(lambda i: part_copy(i).wait_recv())
        total = zero * picked
        values = got[...].reshape(total, piece + LANES)
        lanes = lax.broadcasted_iota(jnp.int32, (total, LANES), 1) * again // LANES
        tags = jnp.where(lanes == me % again, 0.0, values[:, piece:].astype(jnp.float32))
        tags = jnp.max(tags, axis=1, keepdims=True)
        r_at = lax.broadcasted_iota(jnp.int32, (total, LANES), 0) % rank
        l_at = lax.broadcasted_iota(jnp.int32, (total, LANES), 1)
        same = r_at == l_at % rank
        per = LANES // rank
        for e in range(tenants // per):
            targets = (l_at // rank + e * per).astype(jnp.float32)
            member = jnp.where(same & (tags == targets), 1.0, 0.0).astype(jnp.bfloat16)
            sums = lax.dot_general(member, values, TN, preferred_element_type=jnp.float32)
            count = lax.dot_general(
                member, jnp.ones((total, LANES), jnp.bfloat16), TN,
                preferred_element_type=jnp.float32,
            )
            sums = sums / (BLK * count[:, 0:1])
            summed[e * per : (e + 1) * per] = sums.astype(jnp.bfloat16).reshape(per, rank, piece + LANES)
        each(lambda i: final_copy(i).start())
        final[me] = summed[me]

    base(0, 0)
    ready, taken = [], 0
    while turns:
        s, e = turns[0]
        advance()
        taken += 1
        if taken == plan["add"]:
            add_up()
        if e == cuts - 1:
            for d in ready:
                base(d, len(made))
            ready = [d for d in (s + 1, n - 1 - s) if d not in made and s + 1 < n // 2]
    if taken < plan["add"]:
        add_up()
    for d in range(n):
        if d not in made:
            base(d, len(made))

    each(lambda i: final_copy(i).wait_recv())
    for p in range(zero):
        ga[:, p * piece : (p + 1) * piece] = final[p, :, 0:piece].astype(jnp.float32)
    for c in range(kv // LANES):
        total = jnp.zeros((rank, LANES), jnp.float32)
        for e in range(again):
            chunk = final[c * again + e, :, piece : piece + LANES].astype(jnp.float32)
            total = jnp.where(lane[:rank] == e, chunk, total)
        gb[:, c * LANES : (c + 1) * LANES] = total
    ab.end()
    for w in ws:
        w.end()
    each(lambda i: part_copy(i).wait_send())
    each(lambda i: final_copy(i).wait_send())

    def written(i, c):
        cols = pl.ds(pl.multiple_of(i * held, held), held)
        pltpu.make_async_copy(out.at[:, cols], gi.at[:, cols], stored.at[i]).wait()
        return c

    lax.fori_loop(0, zero, written, 0)


def body(features, grad_out, base_weight, factor_a, factor_b, tenant_ids, owner_of):
    zero = lax.axis_size("zero")
    rows, width = features.shape
    kv = grad_out.shape[1]
    rank = factor_a.shape[2]
    held = base_weight.shape[0]
    blocks = rows // BLK
    piece = width // zero
    picked = blocks * rank
    n = zero // 2
    bf16, f32 = jnp.bfloat16, jnp.float32
    vmem = pl.BlockSpec(memory_space=pltpu.VMEM)
    smem = pl.BlockSpec(memory_space=pltpu.SMEM)
    anywhere = pl.BlockSpec(memory_space=pl.ANY)
    dma = pltpu.SemaphoreType.DMA
    grad_in, grad_at, grad_b = pl.pallas_call(
        functools.partial(kernel, zero, PLAN),
        out_shape=(
            jax.ShapeDtypeStruct((rows, width), bf16),
            jax.ShapeDtypeStruct((rank, width), f32),
            jax.ShapeDtypeStruct((rank, kv), f32),
        ),
        in_specs=[
            smem, smem, anywhere, vmem, anywhere, anywhere, anywhere,
        ],
        out_specs=(anywhere, vmem, vmem),
        scratch_shapes=[
            pltpu.VMEM((rows, width), bf16),
            pltpu.VMEM((rows, width), bf16),
            pltpu.VMEM((zero, held, kv), bf16),
            pltpu.VMEM((zero, rank, width + kv), bf16),
            pltpu.VMEM((picked, width), bf16),
            pltpu.VMEM((rows, picked), bf16),
            pltpu.VMEM((zero, picked, piece + LANES), bf16),
            pltpu.VMEM((zero, picked, piece + LANES), bf16),
            pltpu.VMEM((zero, rank, piece + LANES), bf16),
            pltpu.VMEM((zero, rank, piece + LANES), bf16),
            dma((4,)),
            dma((zero,)),
            dma((PLAN["cuts"], 9, n // 2)),
            dma((PLAN["cuts"], 9, n // 2)),
            dma((9, n // 2)),
            dma((9, n // 2)),
            dma((zero,)),
            dma((zero,)),
            dma((zero,)),
            dma((zero,)),
        ],
        compiler_params=pltpu.CompilerParams(
            collective_id=0, has_side_effects=True, vmem_limit_bytes=58 * 2**20
        ),
        cost_estimate=pl.CostEstimate(
            flops=2 * rows * width * (kv + 3 * picked),
            bytes_accessed=2 * (2 * rows * width + width * kv),
            transcendentals=0,
        ),
    )(
        tenant_ids,
        owner_of,
        features,
        grad_out,
        base_weight,
        jnp.swapaxes(factor_a[0], 0, 1),
        factor_b[0],
    )
    return grad_in, jnp.swapaxes(grad_at, 0, 1)[None], grad_b[None]


def solution(mesh):
    placed = (
        P(("groups", "zero"), None),
        P(("groups", "zero"), None),
        P("zero", None),
        P("zero", None, None),
        P("zero", None, None),
        P(("groups", "zero")),
        P(),
    )
    return jax.shard_map(
        body,
        mesh=mesh,
        in_specs=placed,
        out_specs=(
            P(("groups", "zero"), None),
            P(("groups", "zero"), None, None),
            P(("groups", "zero"), None, None),
        ),
        check_vma=False,
    )
```

```python
import functools

import jax
import jax.numpy as jnp
from jax import lax
from jax.experimental import pallas as pl
from jax.experimental.pallas import tpu as pltpu
from jax.sharding import PartitionSpec as P

BLK = 128
LANES = 128
low_rank_scale = 2.0
MESH = pl.DeviceIdType.MESH
NT = (((1,), (1,)), ((), ()))
TN = (((0,), (0,)), ((), ()))
PLAN = {"cuts": 4, "w": (3, 3, 3, 2), "ab": 21, "after": (2, 2, 2, 2), "add": 4}
CW, CCW, ACROSS_CW, ACROSS_CCW, SIB_CW, SIB_CCW, SIB_ACROSS_CW, SIB_ACROSS_CCW, OWN = range(9)


def slot_of(tenant, owner_of):
    owner = owner_of[tenant]

    def count(u, slot):
        return slot + jnp.where((owner_of[u] == owner) & (u < tenant), 1, 0)

    return lax.fori_loop(0, owner_of.shape[0], count, owner)


def chip_at(pos, chips):
    if chips == 8:
        return 2 * pos + (pos // 4) * (15 - 4 * pos)
    return pos


def pos_of(chip, chips):
    if chips == 8:
        z, y = chip // 2, chip % 2
        return z + y * (7 - 2 * z)
    return chip


class Gather:
    def __init__(self, where, region, send, recv):
        self.where, self.region, self.send, self.recv = where, region, send, recv
        self.half = where[-1] // 2
        self.started, self.received = [], set()

    def copy(self, kind, s):
        g, across, r, core, me, sib, n = self.where
        ahead = 1 - 2 * core
        way = -ahead if kind in (CW, ACROSS_CW, SIB_CW, SIB_ACROSS_CW) else ahead
        back = kind in (CCW, SIB_CCW)
        if kind == OWN:
            pos, part, to = r, None, (g, sib)
        elif kind in (CW, CCW):
            pos = r + s * way
            to = (g, chip_at((r - way + n) % n, n) * 2 + core)
        else:
            pos = r + (1 + s) * way
            to = (across, me) if kind in (ACROSS_CW, ACROSS_CCW) else (g, sib)
        if kind in (CW, CCW, SIB_CW, SIB_CCW):
            part = (1 if back else 0) if s == self.half - 1 else 3
        elif kind in (ACROSS_CW, ACROSS_CCW):
            part = 0
        elif kind != OWN:
            part = 2
        ref = self.region(chip_at((pos + n) % n, n) * 2 + core, part)
        return pltpu.make_async_remote_copy(
            src_ref=ref,
            dst_ref=ref,
            send_sem=self.send.at[kind, s],
            recv_sem=self.recv.at[kind, s],
            device_id=to,
            device_id_type=MESH,
        )

    def start(self, kind, s):
        self.copy(kind, s).start()
        self.started.append((kind, s))

    def need(self, kind, s):
        if (kind, s) not in self.received:
            self.received.add((kind, s))
            self.copy(kind, s).wait_recv()

    def begin(self):
        self.start(CW, 0)
        self.start(CCW, 0)
        self.start(OWN, 0)

    def step(self, s):
        last = s == self.half - 1
        for kind in (CW, CCW):
            self.need(kind, s)
            if not last:
                self.start(kind, s + 1)
            if kind == CW or not last:
                self.start(ACROSS_CW + kind, s)
            self.start(SIB_CW + kind, s)
        if s >= 1:
            self.pass_on(s - 1, (CW, CCW))
        if last:
            self.pass_on(s, (CW,))

    def pass_on(self, s, kinds):
        for kind in kinds:
            self.need(ACROSS_CW + kind, s)
            self.start(SIB_ACROSS_CW + kind, s)

    def whole(self, d):
        half, n = self.half, self.where[-1]
        if d == 0:
            needs = [(OWN, 0)]
        elif d == half:
            needs = [(k, half - 1) for k in (CW, CCW, ACROSS_CW, SIB_CW, SIB_CCW, SIB_ACROSS_CW)]
        elif d < half:
            needs = [(k, d - 1) for k in (CW, ACROSS_CW, SIB_CCW, SIB_ACROSS_CCW)]
        else:
            needs = [(k, n - d - 1) for k in (CCW, ACROSS_CCW, SIB_CW, SIB_ACROSS_CW)]
        for need in needs:
            self.need(*need)

    def end(self):
        for kind, s in self.started:
            self.copy(kind, s).wait_send()


def kernel(
    zero, plan, tenant_ids, owner_of, feat_in, go, w_in, at_in, b_in, gi, ga, gb,
    feat, out, wg, abg, a_sel, low, sent, got, summed, final,
    load, stored, w_send, w_recv, ab_send, ab_recv, p_send, p_recv, f_send, f_recv,
):
    g, me = lax.axis_index("groups"), lax.axis_index("zero")
    n = zero // 2
    core = me % 2
    sib = me + 1 - 2 * core
    parity = g % 2
    across = g + 1 - 2 * parity
    r = pos_of(me // 2, n)
    rows, width = feat.shape
    blocks = rows // BLK
    rank = at_in.shape[0]
    kv = b_in.shape[1]
    held = w_in.shape[0]
    picked = blocks * rank
    piece = width // zero
    tenants = zero

    loads = [
        pltpu.make_async_copy(at_in, abg.at[me, :, pl.ds(0, width)], load.at[0]),
        pltpu.make_async_copy(b_in, abg.at[me, :, pl.ds(width, kv)], load.at[1]),
        pltpu.make_async_copy(w_in, wg.at[me], load.at[2]),
        pltpu.make_async_copy(feat_in, feat, load.at[3]),
    ]
    for copy in loads:
        copy.start()

    barrier = pltpu.get_barrier_semaphore()
    pl.semaphore_signal(barrier, inc=1, device_id=(across, me), device_id_type=MESH)

    def greet(i, c):
        pl.semaphore_signal(
            barrier, inc=1, device_id=(g, (me + i) % zero), device_id_type=MESH
        )
        return c

    lax.fori_loop(1, zero, greet, 0)
    pl.semaphore_wait(barrier, zero)

    cuts = min(plan["cuts"], held // 64)
    sub = held // cuts
    w_thirds = [sub * eighths // 128 * 16 for eighths in plan["w"]]
    ab_third = (width + kv) * plan["ab"] // (72 * LANES) * LANES

    def cut(total, third, part, unit):
        if part == 1:
            return pl.ds(third, total - 2 * third)
        if part == 3:
            return pl.ds(pl.multiple_of(parity * third, unit), total - third)
        at = (parity if part == 0 else 1 - parity) * (total - third)
        return pl.ds(pl.multiple_of(at, unit), third)

    def w_region(e, i, part):
        if part is None:
            return wg.at[i, pl.ds(e * sub, sub), :]
        rows_of = cut(sub, w_thirds[e], part, 16)
        return wg.at[i, pl.ds(pl.multiple_of(e * sub + rows_of.start, 16), rows_of.size), :]

    def ab_region(i, part):
        if part is None:
            return abg.at[i]
        return abg.at[i, :, cut(width + kv, ab_third, part, LANES)]

    where = (g, across, r, core, me, sib, n)
    ab = Gather(where, ab_region, ab_send, ab_recv)
    ws = [
        Gather(where, functools.partial(w_region, e), w_send.at[e], w_recv.at[e])
        for e in range(cuts)
    ]

    loads[0].wait()
    loads[1].wait()
    ab.begin()
    loads[2].wait()
    for w in ws:
        w.begin()
    turns = [(s, e) for s in range(n // 2) for e in range(cuts)]
    after = plan["after"]
    for s in range(n // 2):
        ab.step(s)
        for _ in range(after[s] if s < len(after) else 0):
            t, e = turns.pop(0)
            ws[e].step(t)
    for d in range(n):
        ab.whole(d)

    def advance():
        s, e = turns.pop(0)
        ws[e].step(s)

    row = lax.broadcasted_iota(jnp.int32, (rows, picked), 0) // BLK
    col = lax.broadcasted_iota(jnp.int32, (rows, picked), 1) // rank
    mine = row == col
    tag = jnp.zeros((picked, LANES), jnp.float32)
    at = lax.broadcasted_iota(jnp.int32, (picked, LANES), 0) // rank
    b_parts = []
    for k in range(blocks):
        slot = slot_of(tenant_ids[k * BLK], owner_of)
        a_sel[k * rank : (k + 1) * rank, :] = abg[slot, :, 0:width]
        b_parts.append(abg[slot, :, width : width + kv])
        tag = jnp.where(at == k, slot.astype(jnp.float32), tag)
    b_sel = jnp.concatenate(b_parts, axis=0)
    wide = low_rank_scale * lax.dot_general(go[...], b_sel, NT, preferred_element_type=jnp.float32)
    low[...] = jnp.where(mine, wide, 0.0).astype(jnp.bfloat16)
    loads[3].wait()

    def parts(p, inner):
        cols = pl.ds(pl.multiple_of(p * piece, piece), piece)
        x = feat[:, cols]
        part = lax.dot_general(low[...], x, TN, preferred_element_type=jnp.float32)
        sent[p, :, 0:piece] = part.astype(jnp.bfloat16)
        return inner + lax.dot_general(x, a_sel[:, cols], NT, preferred_element_type=jnp.float32)

    inner = lax.fori_loop(0, zero, parts, jnp.zeros((rows, picked), jnp.float32))
    advance()
    inner = jnp.where(mine, inner, 0.0).astype(jnp.bfloat16)
    part_b = low_rank_scale * lax.dot_general(
        inner, go[...], TN, preferred_element_type=jnp.float32
    )
    again = zero // (kv // LANES)
    lane = lax.broadcasted_iota(jnp.int32, (picked, LANES), 1) * again // LANES
    for p in range(zero):
        c = p // again
        chunk = jnp.where(lane == p % again, part_b[:, c * LANES : (c + 1) * LANES], tag)
        sent[p, :, piece : piece + LANES] = chunk.astype(jnp.bfloat16)

    def part_copy(i):
        to = (me + i) % zero
        return pltpu.make_async_remote_copy(
            src_ref=sent.at[to], dst_ref=got.at[me], send_sem=p_send.at[i],
            recv_sem=p_recv.at[i], device_id=(g, to), device_id_type=MESH,
        )

    def final_copy(i):
        to = (me + i) % zero
        return pltpu.make_async_remote_copy(
            src_ref=summed.at[to], dst_ref=final.at[me], send_sem=f_send.at[i],
            recv_sem=f_recv.at[i], device_id=(g, to), device_id_type=MESH,
        )

    def each(act):
        def go_on(i, c):
            act(i)
            return c

        lax.fori_loop(1, zero, go_on, 0)

    each(lambda i: part_copy(i).start())
    got[me] = sent[me]

    made = []

    def base(d, order):
        def one(k, c):
            z = chip_at((r - d * (1 - 2 * core) + n) % n, n) * 2 + k
            cols = pl.ds(pl.multiple_of(z * held, held), held)
            total = lax.dot_general(go[...], wg[z], NT, preferred_element_type=jnp.float32)
            total += jnp.dot(low[...], a_sel[:, cols], preferred_element_type=jnp.float32)
            out[:, cols] = total.astype(jnp.bfloat16)
            pltpu.make_async_copy(out.at[:, cols], gi.at[:, cols], stored.at[2 * order + k]).start()
            return c

        made.append(d)
        for w in ws:
            w.whole(d)
        lax.fori_loop(0, 2, one, 0)

    def add_up():
        each(lambda i: part_copy(i).wait_recv())
        total = zero * picked
        values = got[...].reshape(total, piece + LANES)
        lanes = lax.broadcasted_iota(jnp.int32, (total, LANES), 1) * again // LANES
        tags = jnp.where(lanes == me % again, 0.0, values[:, piece:].astype(jnp.float32))
        tags = jnp.max(tags, axis=1, keepdims=True)
        r_at = lax.broadcasted_iota(jnp.int32, (total, LANES), 0) % rank
        l_at = lax.broadcasted_iota(jnp.int32, (total, LANES), 1)
        same = r_at == l_at % rank
        per = LANES // rank
        for e in range(tenants // per):
            targets = (l_at // rank + e * per).astype(jnp.float32)
            member = jnp.where(same & (tags == targets), 1.0, 0.0).astype(jnp.bfloat16)
            sums = lax.dot_general(member, values, TN, preferred_element_type=jnp.float32)
            count = lax.dot_general(
                member, jnp.ones((total, LANES), jnp.bfloat16), TN,
                preferred_element_type=jnp.float32,
            )
            sums = sums / (BLK * count[:, 0:1])
            summed[e * per : (e + 1) * per] = sums.astype(jnp.bfloat16).reshape(per, rank, piece + LANES)
        each(lambda i: final_copy(i).start())
        final[me] = summed[me]

    base(0, 0)
    ready, taken = [], 0
    while turns:
        s, e = turns[0]
        advance()
        taken += 1
        if taken == plan["add"]:
            add_up()
        if e == cuts - 1:
            for d in ready:
                base(d, len(made))
            ready = [d for d in (s + 1, n - 1 - s) if d not in made and s + 1 < n // 2]
    if taken < plan["add"]:
        add_up()
    for d in range(n):
        if d not in made:
            base(d, len(made))

    each(lambda i: final_copy(i).wait_recv())
    for p in range(zero):
        ga[:, p * piece : (p + 1) * piece] = final[p, :, 0:piece].astype(jnp.float32)
    for c in range(kv // LANES):
        total = jnp.zeros((rank, LANES), jnp.float32)
        for e in range(again):
            chunk = final[c * again + e, :, piece : piece + LANES].astype(jnp.float32)
            total = jnp.where(lane[:rank] == e, chunk, total)
        gb[:, c * LANES : (c + 1) * LANES] = total
    ab.end()
    for w in ws:
        w.end()
    each(lambda i: part_copy(i).wait_send())
    each(lambda i: final_copy(i).wait_send())

    def written(i, c):
        cols = pl.ds(pl.multiple_of(i * held, held), held)
        pltpu.make_async_copy(out.at[:, cols], gi.at[:, cols], stored.at[i]).wait()
        return c

    lax.fori_loop(0, zero, written, 0)


def body(features, grad_out, base_weight, factor_a, factor_b, tenant_ids, owner_of):
    zero = lax.axis_size("zero")
    rows, width = features.shape
    kv = grad_out.shape[1]
    rank = factor_a.shape[2]
    held = base_weight.shape[0]
    blocks = rows // BLK
    piece = width // zero
    picked = blocks * rank
    n = zero // 2
    bf16, f32 = jnp.bfloat16, jnp.float32
    vmem = pl.BlockSpec(memory_space=pltpu.VMEM)
    smem = pl.BlockSpec(memory_space=pltpu.SMEM)
    anywhere = pl.BlockSpec(memory_space=pl.ANY)
    dma = pltpu.SemaphoreType.DMA
    grad_in, grad_at, grad_b = pl.pallas_call(
        functools.partial(kernel, zero, PLAN),
        out_shape=(
            jax.ShapeDtypeStruct((rows, width), bf16),
            jax.ShapeDtypeStruct((rank, width), f32),
            jax.ShapeDtypeStruct((rank, kv), f32),
        ),
        in_specs=[
            smem, smem, anywhere, vmem, anywhere, anywhere, anywhere,
        ],
        out_specs=(anywhere, vmem, vmem),
        scratch_shapes=[
            pltpu.VMEM((rows, width), bf16),
            pltpu.VMEM((rows, width), bf16),
            pltpu.VMEM((zero, held, kv), bf16),
            pltpu.VMEM((zero, rank, width + kv), bf16),
            pltpu.VMEM((picked, width), bf16),
            pltpu.VMEM((rows, picked), bf16),
            pltpu.VMEM((zero, picked, piece + LANES), bf16),
            pltpu.VMEM((zero, picked, piece + LANES), bf16),
            pltpu.VMEM((zero, rank, piece + LANES), bf16),
            pltpu.VMEM((zero, rank, piece + LANES), bf16),
            dma((4,)),
            dma((zero,)),
            dma((PLAN["cuts"], 9, n // 2)),
            dma((PLAN["cuts"], 9, n // 2)),
            dma((9, n // 2)),
            dma((9, n // 2)),
            dma((zero,)),
            dma((zero,)),
            dma((zero,)),
            dma((zero,)),
        ],
        compiler_params=pltpu.CompilerParams(
            collective_id=0, has_side_effects=True, vmem_limit_bytes=58 * 2**20
        ),
        cost_estimate=pl.CostEstimate(
            flops=2 * rows * width * (kv + 3 * picked),
            bytes_accessed=2 * (2 * rows * width + width * kv),
            transcendentals=0,
        ),
    )(
        tenant_ids,
        owner_of,
        features,
        grad_out,
        base_weight,
        jnp.swapaxes(factor_a[0], 0, 1),
        factor_b[0],
    )
    return grad_in, jnp.swapaxes(grad_at, 0, 1)[None], grad_b[None]


def solution(mesh):
    placed = (
        P(("groups", "zero"), None),
        P(("groups", "zero"), None),
        P("zero", None),
        P("zero", None, None),
        P("zero", None, None),
        P(("groups", "zero")),
        P(),
    )
    return jax.shard_map(
        body,
        mesh=mesh,
        in_specs=placed,
        out_specs=(
            P(("groups", "zero"), None),
            P(("groups", "zero"), None, None),
            P(("groups", "zero"), None, None),
        ),
        check_vma=False,
    )
```
